32 devices in a mesh: dp: 8 (over z, y), mp: 4 (over x, core).
Axes of the slice: x: 2, y: 2, z: 4, core: 2. Of those that a mesh axis runs over, the one named last changes fastest.
Arguments:
- tree_query: bfloat16 [1024, 2048], P('dp', 'mp'), may hold values from -6 to 6
- new_kv: bfloat16 [1024, 2, 512], P('dp', None, 'mp'), may hold values from -6 to 6
- kv_cache: bfloat16 [320, 2, 128, 512], P('dp', None, None, 'mp'), may hold values from -4 to 4
- page_table: int32 [16, 32], P('dp'), may hold values from 0 to 39, as said below
- cache_len: int32 [16], P('dp'), may hold values from 2 to 4096, as said below
- tree_mask: int32 [16, 64, 64], P('dp'), may hold values from 0 to 1, as said below
- out_weight: bfloat16 [2048, 2048], P('mp'), may hold values from -0.5 to 0.5
- residual_in: bfloat16 [1024, 2048], P('dp'), may hold values from -3 to 3
- norm_gain: float32 [2048], replicated, may hold values from 0.25 to 1.75
- route_ids: int32 [1024, 6], P('dp'), may hold values from 0 to 7, all different within a row; in each aligned block of 128 rows (0 to 127, 128 to 255, ...) at most 128 rows name the same one
- route_weight: float32 [1024, 6], P('dp'), may hold values from 0.05 to 0.5
- w_gate: bfloat16 [8, 2048, 1408], P('dp', None, 'mp'), may hold values from -0.125 to 0.125
- w_up: bfloat16 [8, 2048, 1408], P('dp', None, 'mp'), may hold values from -0.125 to 0.125
- w_down: bfloat16 [8, 1408, 2048], P('dp', None, 'mp'), may hold values from -0.15625 to 0.15625
- shared_gate: bfloat16 [2048, 2816], P('dp', 'mp'), may hold values from -0.125 to 0.125
- shared_up: bfloat16 [2048, 2816], P('dp', 'mp'), may hold values from -0.125 to 0.125
- shared_down: bfloat16 [2816, 2048], P('mp', 'dp'), may hold values from -0.109375 to 0.109375
Outputs:
- layer_out: bfloat16 [1024, 2048], P('dp', 'mp')
The draws below stay inside these ranges and needn't reach their ends.
Inputs may be any that keep to these rules, and one draw needn't show every extreme that they name: `route_ids`: each row names 6 different experts. Within the rows of one index of dp (aligned blocks of 128 rows) no expert is named by more than 128 rows, and in some block one expert is named by exactly 128 rows. `cache_len`: the pages of the requests of one index of dp number at most 40 together; some request has exactly 4096 cached positions. `page_table`: entry [r, j] is the slot, in the pool of the index of dp that holds request r, of the page with cache positions j * 128 to j * 128 + 127. Entries with j * 128 < cache_len[r] are distinct over the requests of one index of dp; the other entries are valid slots whose contents are not read. tree_mask[r, i, u] is 1 where tree node u is node i or an ancestor of it, else 0; node 0 is the root and each other node's parent has a smaller index.
All inputs are finite; a program needn't handle non-finite values.
Results may differ from the reference program's by a relative error of at most 0.009.
Values may be sent and summed in bfloat16 or wider, within the bound.
A program may use at most 128 MiB of HBM per device.

```python
import math
import jax
import jax.numpy as jnp
import numpy as np
from jax import lax

D = 2048
HEADS = 16
KV_HEADS = 4
HEAD_DIM = 128
FF = 1408
SHARED_FF = 2816
TOPK = 6
PAGE = 128
TREE = 64
MAXPAGES = 32
REQ_DEV = 2
EXPERTS = 8
TOK_DEV = 128
REQUESTS = 16
TOKENS = 1024
PAGES_DEV = 40
CACHE_PAGES = 320
CAP = 128
N_DP = 8


def cache_plan(key):
    groups = REQUESTS // REQ_DEV
    subkeys = jax.random.split(jax.random.fold_in(key, 101), 6)
    levels = int(math.log2(MAXPAGES))
    long_pick = jax.random.randint(subkeys[0], (groups,), 0, REQ_DEV)
    exponents = jax.random.randint(subkeys[1], (groups,), 0, levels + 1)
    long_pages = jnp.left_shift(jnp.ones((groups,), jnp.int32), exponents)
    short_pages = jax.random.randint(subkeys[2], (groups, REQ_DEV), 1, 5)
    is_long = jnp.arange(REQ_DEV)[None, :] == long_pick[:, None]
    page_counts = jnp.where(is_long, long_pages[:, None], short_pages)
    tail_rows = jax.random.randint(subkeys[3], (groups, REQ_DEV), 2, PAGE + 1)
    forced = jax.random.randint(subkeys[4], (), 0, groups)
    full_group = (jnp.arange(groups)[:, None] == forced) & is_long
    page_counts = jnp.where(full_group, MAXPAGES, page_counts)
    tail_rows = jnp.where(full_group, PAGE, tail_rows)
    lengths = (page_counts - 1) * PAGE + tail_rows
    orders = jax.vmap(lambda subkey: jax.random.permutation(subkey, PAGES_DEV))(jax.random.split(subkeys[5], groups))
    offsets = jnp.cumsum(page_counts, axis=1) - page_counts
    columns = (offsets[:, :, None] + jnp.arange(MAXPAGES)[None, None, :]) % PAGES_DEV
    slot_table = jax.vmap(lambda order_row, column_rows: order_row[column_rows])(orders, columns)
    return (lengths.reshape(REQUESTS).astype(jnp.int32), slot_table.reshape(REQUESTS, MAXPAGES).astype(jnp.int32))


def draw_cache_len(key, part):
    return cache_plan(key)[0]


def draw_page_table(key, part):
    return cache_plan(key)[1]


def draw_tree_mask(key, part):
    limits = jnp.maximum(jnp.arange(TREE), 1)
    parents = jax.random.randint(jax.random.fold_in(key, 303), (REQUESTS, TREE), 0, limits[None, :])
    identity_rows = jnp.eye(TREE, dtype=jnp.int32)

    def add_node(node, ancestors):
        parent_rows = jax.vmap(lambda table_rows, parent: table_rows[parent])(ancestors, parents[:, node])
        parent_rows = jnp.where(node > 0, parent_rows, 0)
        new_row = jnp.maximum(parent_rows, identity_rows[node][None, :])
        return ancestors.at[:, node, :].set(new_row)
    ancestors = lax.fori_loop(0, TREE, add_node, jnp.zeros((REQUESTS, TREE, TREE), jnp.int32))
    return ancestors.astype(jnp.int32)


def draw_tree_query(key, part):
    shape = (TOKENS, HEADS * HEAD_DIM)
    values = jnp.clip(1.5 * jax.random.normal(jax.random.fold_in(key, 11), shape), -6.0, 6.0)
    return values.astype(jnp.bfloat16)


def draw_new_kv(key, part):
    shape = (TOKENS, 2, KV_HEADS * HEAD_DIM)
    values = jnp.clip(jax.random.normal(jax.random.fold_in(key, 13), shape), -4.0, 4.0)
    return values.astype(jnp.bfloat16)


def level_of(key, shape, cuts, low, high):
    loudness, own = 1.0, jax.random.fold_in(key, 6)
    for dim, parts in cuts:
        draws = jnp.exp(jax.random.uniform(jax.random.fold_in(own, dim), (parts,), jnp.float32, low / len(cuts), high / len(cuts)))
        loudness = loudness * jnp.repeat(draws, shape[dim] // parts).reshape([-1 if axis == dim else 1 for axis in range(len(shape))])
    return loudness


def deal_out(stream_key, own, number, rows, number_of, top, bound, lean):
    sequence = jax.random.permutation(stream_key, number_of)
    packed, ordinary = shares(number_of, rows * top, bound, lean, True), shares(number_of, rows * top, bound, lean, False)
    places = jnp.arange(number_of)

    def named(tallies, turn):
        used = int((tallies > 0).sum())
        fixed = max(1, used // 4)
        moved = fixed + (places - fixed + turn * (used - fixed)) % max(1, number_of - fixed)
        return jnp.zeros((number_of,), jnp.int32).at[sequence[jnp.where(places < fixed, places, moved)]].set(jnp.asarray(tallies, jnp.int32))

    tallies = jnp.where(number % 4 == 0, named(packed, number // 4), named(ordinary, number - number // 4 - 1))
    mixed = jax.random.permutation(jax.random.fold_in(own, 3), number_of)
    donor, taker = mixed[0:number_of // 2 * 2:2], mixed[1:number_of // 2 * 2:2]
    slack = jnp.minimum(tallies[donor] - 1, bound - tallies[taker]) // 2
    slack = jnp.where((donor == sequence[0]) | (taker == sequence[0]) | (tallies[taker] == 0), 0, jnp.maximum(slack, 0))
    moved = jax.random.randint(jax.random.fold_in(own, 4), (number_of // 2,), 0, 1 << 20) % (slack + 1)
    tallies = tallies.at[donor].add(-moved).at[taker].add(moved)
    items = jnp.searchsorted(jnp.cumsum(tallies), jnp.arange(rows * top), side="right").astype(jnp.int32)
    listing = items.reshape(top, rows).T
    listing = listing[jax.random.permutation(jax.random.fold_in(own, 1), rows)]
    turn = jax.random.randint(jax.random.fold_in(own, 2), (rows, 1), 0, top)
    return jnp.take_along_axis(listing, (jnp.arange(top)[None, :] + turn) % top, axis=1)


def shares(count, total, reach, lean, full):
    loads = [(1 << 20) // math.isqrt(grade ** lean) + 1 for grade in range(1, count + 1)]
    largest = reach if full else min(reach, max(-(-total // count), total * loads[0] // sum(loads)))
    least = 1 if total - largest >= count - 1 else 0
    given, surplus = [largest] + [least] * (count - 1), total - largest - least * (count - 1)
    while surplus > 0:
        movable = [i for i in range(1, count) if given[i] < largest] or [i for i in range(1, count) if given[i] < reach]
        pool, left = sum([loads[i] for i in movable]), surplus
        for i in movable:
            extra = min(reach - given[i], max(1, left * loads[i] // pool), surplus)
            given[i] = given[i] + extra
            surplus = surplus - extra
    return np.array(given)


def normal_values(stream_key, extent, spread, reach, cuts=(), kind=jnp.bfloat16):
    drawn = spread * jax.random.normal(stream_key, extent, jnp.float32)
    if cuts:
        drawn = drawn * level_of(stream_key, extent, cuts, -0.22, 0.18)
    return jnp.clip(drawn, -reach, reach).astype(kind)


def setup_inputs(seed: int = 0) -> dict:
    keys = jax.random.split(jax.random.key(seed), 18)
    tree_query = draw_tree_query(jax.random.fold_in(keys[17], 71), 0)
    new_kv = draw_new_kv(jax.random.fold_in(keys[17], 71), 0)
    kv_cache = normal_values(keys[2], (CACHE_PAGES, 2, PAGE, KV_HEADS * HEAD_DIM), 1.0, 4.0, ((0, 8), (3, 4)))
    page_table = draw_page_table(jax.random.fold_in(keys[17], 71), 0)
    cache_len = draw_cache_len(jax.random.fold_in(keys[17], 71), 0)
    tree_mask = draw_tree_mask(jax.random.fold_in(keys[17], 71), 0)
    out_weight = normal_values(keys[6], (HEADS * HEAD_DIM, D), (HEADS * HEAD_DIM // 16) ** -0.5, 0.5, ((0, 4),))
    residual_in = normal_values(keys[7], (TOKENS, D), 0.5, 3.0, ((0, 8),))
    norm_gain = jnp.clip(1.0 + 0.15 * jax.random.normal(keys[8], (D,), jnp.float32), 0.25, 1.75)
    route_ids_keys = jax.random.split(jax.random.fold_in(keys[9], 1), TOKENS // TOK_DEV)
    route_ids_turns = jax.random.permutation(jax.random.fold_in(keys[9], 3), TOKENS // TOK_DEV)
    route_ids = jax.vmap(lambda own, number: deal_out(jax.random.fold_in(keys[9], 2), own, number, TOK_DEV, EXPERTS, TOPK, CAP, 2))(route_ids_keys, route_ids_turns).reshape((TOKENS, TOPK))
    route_weight = jnp.clip(jnp.exp(math.log(0.5) - 2.3025851 * jax.random.uniform(keys[10], (TOKENS, TOPK), jnp.float32) ** level_of(keys[10], (TOKENS, TOPK), ((0, 8),), -0.2, 0.2)), 0.05, 0.5)
    w_gate = normal_values(keys[11], (EXPERTS, D, FF), D ** -0.5, 0.125, ((0, 8), (2, 4)))
    w_up = normal_values(keys[12], (EXPERTS, D, FF), D ** -0.5, 0.125, ((0, 8), (2, 4)))
    w_down = normal_values(keys[13], (EXPERTS, FF, D), FF ** -0.5, 0.15625, ((0, 8), (2, 4)))
    shared_gate = normal_values(keys[14], (D, SHARED_FF), D ** -0.5, 0.125, ((0, 8), (1, 4)))
    shared_up = normal_values(keys[15], (D, SHARED_FF), D ** -0.5, 0.125, ((0, 8), (1, 4)))
    shared_down = normal_values(keys[16], (SHARED_FF, D), SHARED_FF ** -0.5, 0.109375, ((0, 4), (1, 8)))
    return dict(tree_query=tree_query, new_kv=new_kv, kv_cache=kv_cache, page_table=page_table, cache_len=cache_len, tree_mask=tree_mask, out_weight=out_weight, residual_in=residual_in, norm_gain=norm_gain, route_ids=route_ids, route_weight=route_weight, w_gate=w_gate, w_up=w_up, w_down=w_down, shared_gate=shared_gate, shared_up=shared_up, shared_down=shared_down)


NEGATIVE_FILL = -1e+30
EPSILON = 1e-05

def normalize(rows, gain):
    values = rows.astype(jnp.float32)
    mean_square = lax.optimization_barrier(jnp.mean(values * values, axis=-1, keepdims=True))
    return (values * lax.rsqrt(mean_square + EPSILON) * gain).astype(jnp.bfloat16)

def reference(tree_query, new_kv, kv_cache, page_table, cache_len, tree_mask, out_weight, residual_in, norm_gain, route_ids, route_weight, w_gate, w_up, w_down, shared_gate, shared_up, shared_down):
    group_size = HEADS // KV_HEADS
    score_scale = HEAD_DIM ** (-0.5)

    def per_request(request):
        pool_base = request // REQ_DEV * PAGES_DEV
        kv_pages = kv_cache[pool_base + page_table[request]]
        cache_keys = kv_pages[:, 0].reshape(MAXPAGES * PAGE, KV_HEADS, HEAD_DIM).astype(jnp.float32)
        cache_values = kv_pages[:, 1].reshape(MAXPAGES * PAGE, KV_HEADS, HEAD_DIM).astype(jnp.float32)
        q_rows = lax.dynamic_slice_in_dim(tree_query, request * TREE, TREE, 0)
        q_rows = q_rows.reshape(TREE, KV_HEADS, group_size, HEAD_DIM).astype(jnp.float32)
        fresh_rows = lax.dynamic_slice_in_dim(new_kv, request * TREE, TREE, 0).astype(jnp.float32)
        tree_keys = fresh_rows[:, 0].reshape(TREE, KV_HEADS, HEAD_DIM)
        tree_values = fresh_rows[:, 1].reshape(TREE, KV_HEADS, HEAD_DIM)
        live_mask = jnp.arange(MAXPAGES * PAGE, dtype=jnp.int32) < cache_len[request]
        cache_scores = jnp.einsum('tgjd,kgd->gjtk', q_rows, cache_keys) * score_scale
        cache_scores = jnp.where(live_mask, cache_scores, NEGATIVE_FILL)
        tree_allow = tree_mask[request] == 1
        tree_scores = jnp.einsum('tgjd,ugd->gjtu', q_rows, tree_keys) * score_scale
        tree_scores = jnp.where(tree_allow, tree_scores, NEGATIVE_FILL)
        row_peak = jnp.maximum(lax.optimization_barrier(jnp.max(cache_scores, axis=-1)), lax.optimization_barrier(jnp.max(tree_scores, axis=-1)))[..., None]
        cache_probs = jnp.where(live_mask, jnp.exp(cache_scores - row_peak), 0.0)
        tree_probs = jnp.where(tree_allow, jnp.exp(tree_scores - row_peak), 0.0)
        denom_sum = lax.optimization_barrier(jnp.sum(cache_probs, axis=-1)) + lax.optimization_barrier(jnp.sum(tree_probs, axis=-1))
        cache_weights = lax.optimization_barrier(cache_probs.astype(jnp.bfloat16)).astype(jnp.float32)
        tree_weights = lax.optimization_barrier(tree_probs.astype(jnp.bfloat16)).astype(jnp.float32)
        weighted = jnp.einsum('gjtk,kgd->tgjd', cache_weights, cache_values)
        weighted = weighted + jnp.einsum('gjtu,ugd->tgjd', tree_weights, tree_values)
        result = weighted / jnp.transpose(denom_sum, (2, 0, 1))[..., None]
        return result.reshape(TREE, HEADS * HEAD_DIM).astype(jnp.bfloat16)
    attended = lax.map(per_request, jnp.arange(REQUESTS, dtype=jnp.int32)).reshape(TOKENS, HEADS * HEAD_DIM)
    projected = jnp.dot(attended, out_weight, preferred_element_type=jnp.float32)
    stream = (residual_in.astype(jnp.float32) + projected).astype(jnp.bfloat16)
    normed = normalize(stream, norm_gain)
    shared_gate_proj = jnp.dot(normed, shared_gate, preferred_element_type=jnp.float32)
    shared_up_proj = jnp.dot(normed, shared_up, preferred_element_type=jnp.float32)
    shared_hidden = (jax.nn.silu(shared_gate_proj) * shared_up_proj).astype(jnp.bfloat16)
    shared_out = jnp.dot(shared_hidden, shared_down, preferred_element_type=jnp.float32).astype(jnp.bfloat16)
    shared_out = lax.optimization_barrier(shared_out).astype(jnp.float32)
    block_ids = route_ids.reshape(N_DP, TOK_DEV * TOPK)
    onehot = (block_ids[..., None] == jnp.arange(EXPERTS, dtype=jnp.int32)).astype(jnp.int32)
    slot_index = lax.optimization_barrier(jnp.sum((jnp.cumsum(onehot, axis=1) - onehot) * onehot, axis=-1))
    columns = (jnp.arange(N_DP, dtype=jnp.int32)[:, None] * CAP + slot_index).reshape(-1)
    token_of = jnp.arange(TOKENS * TOPK, dtype=jnp.int32) // TOPK
    flat_ids = route_ids.reshape(-1)
    token_table = jnp.full((EXPERTS, N_DP * CAP), TOKENS, jnp.int32).at[flat_ids, columns].set(token_of)
    weight_table = jnp.zeros((EXPERTS, N_DP * CAP), jnp.float32).at[flat_ids, columns].set(route_weight.reshape(-1))
    padded = jnp.concatenate([normed, jnp.zeros((1, D), jnp.bfloat16)], axis=0)

    def expert_step(running, expert_item):
        gate_e, up_e, down_e, token_rows, weights = expert_item
        rows = padded[token_rows]
        gate_proj = jnp.dot(rows, gate_e, preferred_element_type=jnp.float32)
        up_proj = jnp.dot(rows, up_e, preferred_element_type=jnp.float32)
        hidden_act = (jax.nn.silu(gate_proj) * up_proj).astype(jnp.bfloat16)
        expert_out = jnp.dot(hidden_act, down_e, preferred_element_type=jnp.float32).astype(jnp.bfloat16)
        expert_out = lax.optimization_barrier(expert_out).astype(jnp.float32)
        running = running.at[token_rows].add(weights[:, None] * expert_out, mode='drop')
        return (running, None)
    mixture, _ = lax.scan(expert_step, jnp.zeros((TOKENS, D), jnp.float32), (w_gate, w_up, w_down, token_table, weight_table))
    return (stream.astype(jnp.float32) + shared_out + mixture).astype(jnp.bfloat16)
```

```python
import functools

import jax
import jax.numpy as jnp
from jax import lax
from jax.experimental import pallas as pl
from jax.experimental.pallas import tpu as pltpu
from jax.sharding import PartitionSpec as P

MESH = pl.DeviceIdType.MESH

NEGATIVE_FILL = -1e30
EPSILON = 1e-05
LOG2_E = 1.4426950408889634


def normalize(rows, gain):
    values = rows.astype(jnp.float32)
    mean_square = jnp.mean(values * values, axis=-1, keepdims=True)
    return (values * lax.rsqrt(mean_square + EPSILON) * gain).astype(jnp.bfloat16)


def attend_kernel(
    heads,
    group,
    score_scale,
    table_ref,
    length_ref,
    query_ref,
    fresh_ref,
    mask_ref,
    cache_ref,
    weight_ref,
    out_ref,
    attended,
):
    req_count, tree_len = mask_ref.shape[0], mask_ref.shape[1]
    page, dim = cache_ref.shape[2], cache_ref.shape[3]
    factor = score_scale * LOG2_E
    contract = (((1,), (1,)), ((), ()))
    for r in range(req_count):
        tokens = slice(r * tree_len, (r + 1) * tree_len)
        queries = jnp.concatenate(
            [query_ref[tokens, h * dim : (h + 1) * dim] for h in range(heads)], axis=0
        )
        allow = jnp.concatenate([mask_ref[r]] * heads, axis=0) == 1
        scores = (
            lax.dot_general(
                queries, fresh_ref[tokens, :dim], contract, preferred_element_type=jnp.float32
            )
            * factor
        )
        scores = jnp.where(allow, scores, NEGATIVE_FILL)
        peak = jnp.max(scores, axis=1, keepdims=True)
        probs = jnp.where(allow, jnp.exp2(scores - peak), 0.0)
        denom = jnp.sum(probs, axis=1, keepdims=True)
        weighted = jnp.dot(
            probs.astype(jnp.bfloat16),
            fresh_ref[tokens, dim:],
            preferred_element_type=jnp.float32,
        )
        length = length_ref[r]

        def step(j, carry):
            peak, denom, weighted = carry
            slots = [table_ref[r, j * group + i] for i in range(group)]
            keys = jnp.concatenate([cache_ref[slot, 0] for slot in slots], axis=0)
            values = jnp.concatenate([cache_ref[slot, 1] for slot in slots], axis=0)
            scores = (
                lax.dot_general(queries, keys, contract, preferred_element_type=jnp.float32)
                * factor
            )
            places = lax.broadcasted_iota(jnp.int32, (1, group * page), 1) + j * (group * page)
            scores = jnp.where(places < length, scores, NEGATIVE_FILL)
            new_peak = jnp.maximum(peak, jnp.max(scores, axis=1, keepdims=True))
            probs = jnp.exp2(scores - new_peak)
            shrink = jnp.exp2(peak - new_peak)
            denom = denom * shrink + jnp.sum(probs, axis=1, keepdims=True)
            weighted = weighted * shrink + jnp.dot(
                probs.astype(jnp.bfloat16), values, preferred_element_type=jnp.float32
            )
            return new_peak, denom, weighted

        steps = (length + group * page - 1) // (group * page)
        peak, denom, weighted = lax.fori_loop(0, steps, step, (peak, denom, weighted))
        result = (weighted / denom).astype(jnp.bfloat16)
        for h in range(heads):
            attended[tokens, h * dim : (h + 1) * dim] = result[h * tree_len : (h + 1) * tree_len]
    out_ref[...] = jnp.dot(
        attended[...], weight_ref[...], preferred_element_type=jnp.float32
    ).astype(out_ref.dtype)


def attend(
    tree_query, new_kv, kv_cache, page_table, cache_len, tree_mask, out_weight, out_dtype
):
    tok_rows, dim = tree_query.shape[0], new_kv.shape[2]
    heads = tree_query.shape[1] // dim
    group = 4 if page_table.shape[1] % 4 == 0 else 1
    vmem, smem = pl.BlockSpec(memory_space=pltpu.VMEM), pl.BlockSpec(memory_space=pltpu.SMEM)
    return pl.pallas_call(
        functools.partial(attend_kernel, heads, group, dim ** (-0.5)),
        out_shape=jax.ShapeDtypeStruct((tok_rows, out_weight.shape[1]), out_dtype),
        in_specs=[smem, smem, vmem, vmem, vmem, vmem, vmem],
        out_specs=vmem,
        scratch_shapes=[pltpu.VMEM(tree_query.shape, jnp.bfloat16)],
        compiler_params=pltpu.CompilerParams(vmem_limit_bytes=24 * 1024 * 1024),
        cost_estimate=pl.CostEstimate(
            flops=1_000_000_000, bytes_accessed=6_000_000, transcendentals=1_200_000
        ),
        name="attend",
    )(
        page_table,
        cache_len,
        tree_query,
        new_kv.reshape(tok_rows, 2 * dim),
        tree_mask,
        kv_cache,
        out_weight,
    )


def run_experts(rows, w_gate, w_up, w_down):
    source_count, slot_count, model_width = rows.shape
    flat_rows = rows.reshape(source_count * slot_count, model_width)
    gate_proj = jnp.dot(flat_rows, w_gate[0], preferred_element_type=jnp.float32)
    up_proj = jnp.dot(flat_rows, w_up[0], preferred_element_type=jnp.float32)
    hidden_act = (jax.nn.silu(gate_proj) * up_proj).astype(jnp.bfloat16)
    down_rows = w_down[0]
    summed = jnp.dot(
        lax.all_gather(hidden_act, "mp", axis=1, tiled=True),
        down_rows,
        preferred_element_type=jnp.float32,
    )
    outputs = summed.astype(jnp.bfloat16).reshape(source_count, slot_count, w_down.shape[2])
    return lax.all_to_all(outputs, "dp", split_axis=0, concat_axis=0, tiled=True)


def shared_experts(normed_rows, shared_gate, shared_up, shared_down):
    gate_total = jnp.dot(
        normed_rows,
        lax.all_gather(shared_gate, "dp", axis=0, tiled=True),
        preferred_element_type=jnp.float32,
    )
    up_total = jnp.dot(
        normed_rows,
        lax.all_gather(shared_up, "dp", axis=0, tiled=True),
        preferred_element_type=jnp.float32,
    )
    shared_hidden = (jax.nn.silu(gate_total) * up_total).astype(jnp.bfloat16)
    terms = jnp.dot(
        shared_hidden,
        lax.all_gather(shared_down, "dp", axis=1, tiled=True),
        preferred_element_type=jnp.float32,
    )
    return lax.psum_scatter(terms.astype(jnp.bfloat16), "mp", scatter_dimension=1, tiled=True)


def mp_relations(m):
    x, c = m // 2, m % 2
    return (x * 2 + (1 - c), (1 - x) * 2 + c, (1 - x) * 2 + (1 - c))


def remote(src, dst, send, recv, device):
    return pltpu.make_async_remote_copy(
        src_ref=src, dst_ref=dst, send_sem=send, recv_sem=recv, device_id=device, device_id_type=MESH
    )


def greet(devices):
    barrier = pltpu.get_barrier_semaphore()
    for device in devices:
        pl.semaphore_signal(barrier, inc=1, device_id=device, device_id_type=MESH)
    pl.semaphore_wait(barrier, len(devices))


def norm_gather_kernel(
    n_dp,
    partial_ref,
    residual_ref,
    gain_ref,
    rows_ref,
    stream_ref,
    terms,
    stream_own,
    normed_own,
    rs_send,
    rs_recv,
    st_send,
    st_recv,
    dp_send,
    dp_recv,
    x_send,
    x_recv,
    c_send,
    c_recv,
    r_send,
    r_recv,
    local_sem,
):
    d, m = lax.axis_index("dp"), lax.axis_index("mp")
    mates = mp_relations(m)
    core_mate, x_mate = mates[0], mates[1]
    peers = [lax.rem(d + k, n_dp) for k in range(1, n_dp)]
    greet([(d, mate) for mate in mates] + [(peer, m) for peer in peers])
    quarter = stream_own.shape[2]
    rs_copies = [
        remote(partial_ref.at[mate], terms.at[i], rs_send.at[i], rs_recv.at[i], (d, mate))
        for i, mate in enumerate(mates)
    ]
    for copy in (rs_copies[1], rs_copies[2], rs_copies[0]):
        copy.start()
    total = residual_ref[...].astype(jnp.float32) + partial_ref[m].astype(jnp.float32)
    for i, copy in enumerate(rs_copies):
        copy.wait_recv()
        total = total + terms[i].astype(jnp.float32)
    stream = total.astype(jnp.bfloat16)
    values = stream.astype(jnp.float32)
    mean_square = jnp.mean(values * values, axis=-1, keepdims=True)
    normed_own[...] = (values * lax.rsqrt(mean_square + EPSILON) * gain_ref[...]).astype(
        jnp.bfloat16
    )
    for i in range(4):
        stream_own[i] = stream[:, i * quarter : (i + 1) * quarter]
    dp_copies = [
        remote(normed_own, rows_ref.at[d, m], dp_send.at[k], dp_recv.at[k], (peers[k], m))
        for k in range(n_dp - 1)
    ]
    for copy in dp_copies:
        copy.start()
    x_copies, c_copies, r_copies = [], [], []

    def forward(k, source):
        owner = lax.rem(d + n_dp - k, n_dp)
        x_copy = remote(source, rows_ref.at[owner, m], x_send.at[k], x_recv.at[k], (d, x_mate))
        c_copy = remote(source, rows_ref.at[owner, m], c_send.at[k], c_recv.at[k], (d, core_mate))
        x_copy.start()
        c_copy.start()
        x_copies.append(x_copy)
        c_copies.append(c_copy)

    def relay(k):
        owner = lax.rem(d + n_dp - k, n_dp)
        x_copies[k].wait_recv()
        block = rows_ref.at[owner, x_mate]
        copy = remote(block, block, r_send.at[k], r_recv.at[k], (d, core_mate))
        copy.start()
        r_copies.append(copy)

    forward(0, normed_own)
    own_rows = pltpu.make_async_copy(normed_own, rows_ref.at[d, m], local_sem.at[0])
    own_rows.start()
    own_stream = pltpu.make_async_copy(stream_own.at[m], stream_ref.at[m], local_sem.at[1])
    own_stream.start()
    st_copies = [
        remote(stream_own.at[mate], stream_ref.at[m], st_send.at[i], st_recv.at[i], (d, mate))
        for i, mate in enumerate(mates)
    ]
    for copy in st_copies:
        copy.start()
    for k in range(1, n_dp):
        dp_copies[k - 1].wait_recv()
        forward(k, rows_ref.at[lax.rem(d + n_dp - k, n_dp), m])
        relay(k - 1)
    relay(n_dp - 1)
    own_rows.wait()
    own_stream.wait()
    for copy in rs_copies + dp_copies + x_copies:
        copy.wait_send()
    for copy in st_copies + c_copies + r_copies:
        copy.wait()


def norm_gather(n_dp, partial, residual, gain):
    rows, width = residual.shape
    dma = pltpu.SemaphoreType.DMA
    return pl.pallas_call(
        functools.partial(norm_gather_kernel, n_dp),
        out_shape=(
            jax.ShapeDtypeStruct((n_dp, 4, rows, width), jnp.bfloat16),
            jax.ShapeDtypeStruct((4, rows, width // 4), jnp.bfloat16),
        ),
        in_specs=[pl.BlockSpec(memory_space=pltpu.VMEM)] * 3,
        out_specs=(pl.BlockSpec(memory_space=pl.ANY),) * 2,
        scratch_shapes=[
            pltpu.VMEM((3, rows, width), jnp.bfloat16),
            pltpu.VMEM((4, rows, width // 4), jnp.bfloat16),
            pltpu.VMEM((rows, width), jnp.bfloat16),
            dma((3,)),
            dma((3,)),
            dma((3,)),
            dma((3,)),
            dma((n_dp - 1,)),
            dma((n_dp - 1,)),
            dma((n_dp,)),
            dma((n_dp,)),
            dma((n_dp,)),
            dma((n_dp,)),
            dma((n_dp,)),
            dma((n_dp,)),
            dma((2,)),
        ],
        compiler_params=pltpu.CompilerParams(
            collective_id=0, has_side_effects=True, vmem_limit_bytes=16 * 1024 * 1024
        ),
        name="norm_gather",
    )(partial, residual, gain)


def hidden_gather_kernel(
    chunks, own_ref, all_ref, x_send, x_recv, c_send, c_recv, r_send, r_recv, local_sem
):
    d, m = lax.axis_index("dp"), lax.axis_index("mp")
    core_mate, x_mate, _ = mp_relations(m)
    greet([(d, core_mate), (d, x_mate)])
    x_copies = [
        remote(own_ref.at[k], all_ref.at[m, k], x_send.at[k], x_recv.at[k], (d, x_mate))
        for k in range(chunks)
    ]
    c_copies = [
        remote(own_ref.at[k], all_ref.at[m, k], c_send.at[k], c_recv.at[k], (d, core_mate))
        for k in range(chunks)
    ]
    for copy in x_copies + c_copies:
        copy.start()
    local = pltpu.make_async_copy(own_ref, all_ref.at[m], local_sem)
    local.start()
    r_copies = []
    for k in range(chunks):
        x_copies[k].wait_recv()
        block = all_ref.at[x_mate, k]
        copy = remote(block, block, r_send.at[k], r_recv.at[k], (d, core_mate))
        copy.start()
        r_copies.append(copy)
    local.wait()
    for copy in x_copies:
        copy.wait_send()
    for copy in c_copies + r_copies:
        copy.wait()


def hidden_gather(own):
    chunks, rows, width = own.shape
    return pl.pallas_call(
        functools.partial(hidden_gather_kernel, chunks),
        out_shape=jax.ShapeDtypeStruct((4, chunks, rows, width), own.dtype),
        in_specs=[pl.BlockSpec(memory_space=pl.ANY)],
        out_specs=pl.BlockSpec(memory_space=pl.ANY),
        scratch_shapes=[pltpu.SemaphoreType.DMA((chunks,))] * 6 + [pltpu.SemaphoreType.DMA],
        compiler_params=pltpu.CompilerParams(collective_id=1, has_side_effects=True),
        name="hidden_gather",
    )(own)


def combine_kernel(n_dp, own_ref, all_ref, send, recv, local_sem):
    d, m = lax.axis_index("dp"), lax.axis_index("mp")
    peers = [lax.rem(d + k, n_dp) for k in range(1, n_dp)]
    greet([(peer, m) for peer in peers])
    copies = [
        remote(own_ref.at[peers[k]], all_ref.at[d], send.at[k], recv.at[k], (peers[k], m))
        for k in range(n_dp - 1)
    ]
    for copy in copies:
        copy.start()
    local = pltpu.make_async_copy(own_ref.at[d], all_ref.at[d], local_sem)
    local.start()
    local.wait()
    for copy in copies:
        copy.wait()


def combine(own):
    n_dp = own.shape[0]
    return pl.pallas_call(
        functools.partial(combine_kernel, n_dp),
        out_shape=jax.ShapeDtypeStruct(own.shape, own.dtype),
        in_specs=[pl.BlockSpec(memory_space=pl.ANY)],
        out_specs=pl.BlockSpec(memory_space=pl.ANY),
        scratch_shapes=[pltpu.SemaphoreType.DMA((n_dp - 1,))] * 2 + [pltpu.SemaphoreType.DMA],
        compiler_params=pltpu.CompilerParams(collective_id=2, has_side_effects=True),
        name="combine",
    )(own)


def shared_slices(shared_gate, shared_up, shared_down):
    n_dp = lax.axis_size("dp")
    depth, units = shared_gate.shape
    share = units // n_dp
    parts = jnp.concatenate(
        [
            shared_gate.T.reshape(n_dp, share, depth),
            shared_up.T.reshape(n_dp, share, depth),
            shared_down.reshape(n_dp, share, depth),
        ],
        axis=1,
    )
    parts = lax.all_to_all(parts, "dp", split_axis=0, concat_axis=0, tiled=True)
    parts = parts.transpose(1, 0, 2).reshape(3, share, n_dp * depth)
    down = parts[2].reshape(share, 4, -1).transpose(1, 0, 2)
    down = lax.all_to_all(down, "mp", split_axis=0, concat_axis=0, tiled=True)
    return parts[0].T, parts[1].T, down


def dense_tail(
    partial_value,
    residual_in,
    norm_gain,
    route_ids,
    route_weight,
    w_gate,
    w_up,
    w_down,
    shared_gate,
    shared_up,
    shared_down,
):
    n_dp = lax.axis_size("dp")
    tok_rows, model_width = residual_in.shape
    units = w_gate.shape[2]
    own_gate, own_up, own_down = shared_slices(shared_gate, shared_up, shared_down)
    share = own_gate.shape[1]
    width = -(-(units + share) // 128) * 128
    spare = width - units - share
    columns_pad = jnp.zeros((model_width, spare), jnp.bfloat16)
    gate_all = jnp.concatenate([w_gate[0], own_gate, columns_pad], axis=1)
    up_all = jnp.concatenate([w_up[0], own_up, columns_pad], axis=1)
    down_width = w_down.shape[2]
    down_all = jnp.concatenate(
        [
            w_down[0].reshape(4, units, down_width),
            own_down,
            jnp.zeros((4, spare, down_width), jnp.bfloat16),
        ],
        axis=1,
    ).reshape(4 * width, down_width)
    chosen = route_ids[None, :, :] == jnp.arange(n_dp, dtype=jnp.int32)[:, None, None]
    by_expert = jnp.sum(jnp.where(chosen, route_weight[None], 0.0), axis=2)
    row_scale = lax.all_to_all(by_expert, "dp", split_axis=0, concat_axis=0, tiled=True)
    row_scale = row_scale.reshape(n_dp * tok_rows, 1)
    slice_rows = tok_rows // 4
    own_start = lax.axis_index("mp") * slice_rows
    rows, stream = norm_gather(
        n_dp,
        partial_value.reshape(4, slice_rows, model_width),
        lax.dynamic_slice_in_dim(residual_in, own_start, slice_rows, 0),
        norm_gain.reshape(1, model_width),
    )
    rows = rows.reshape(n_dp * tok_rows, model_width)
    gate_proj = jnp.dot(rows, gate_all, preferred_element_type=jnp.float32)
    up_proj = jnp.dot(rows, up_all, preferred_element_type=jnp.float32)
    routed = jnp.arange(width) < units
    scale = jnp.where(routed[None, :], row_scale, 1.0)
    hidden = (jax.nn.silu(gate_proj) * up_proj * scale).astype(jnp.bfloat16)
    hidden = hidden_gather(hidden.reshape(n_dp, tok_rows, width))
    hidden = hidden.reshape(4, n_dp * tok_rows, width)
    outputs = jnp.einsum(
        "mtk,mkc->tc",
        hidden,
        down_all.reshape(4, width, down_width),
        preferred_element_type=jnp.float32,
    )
    terms = combine(outputs.astype(jnp.bfloat16).reshape(n_dp, tok_rows, down_width))
    total = stream.reshape(tok_rows, down_width).astype(jnp.float32)
    return (total + jnp.sum(terms.astype(jnp.float32), axis=0)).astype(jnp.bfloat16)


def on_device(
    tree_query,
    new_kv,
    kv_cache,
    page_table,
    cache_len,
    tree_mask,
    out_weight,
    residual_in,
    norm_gain,
    route_ids,
    route_weight,
    w_gate,
    w_up,
    w_down,
    shared_gate,
    shared_up,
    shared_down,
):
    tok_rows = tree_query.shape[0]
    experts = lax.axis_size("dp") * w_gate.shape[0]
    route_count = route_ids.shape[1]
    capacity = min(tok_rows, 4 * tok_rows * route_count // (3 * experts))
    every_row = capacity == tok_rows and w_gate.shape[0] == 1 and lax.axis_size("mp") == 4
    partial_value = attend(
        tree_query,
        new_kv,
        kv_cache,
        page_table,
        cache_len,
        tree_mask,
        out_weight,
        jnp.bfloat16 if every_row else jnp.float32,
    )
    model_width = residual_in.shape[1]
    quarter = model_width // lax.axis_size("mp")
    col_start = lax.axis_index("mp") * quarter
    if every_row:
        return dense_tail(
            partial_value,
            residual_in,
            norm_gain,
            route_ids,
            route_weight,
            w_gate,
            w_up,
            w_down,
            shared_gate,
            shared_up,
            shared_down,
        )
    expert_ids = route_ids.reshape(-1)
    onehot = expert_ids[:, None] == jnp.arange(experts, dtype=jnp.int32)[None, :]
    onehot = onehot.astype(jnp.bfloat16)
    places = jnp.arange(expert_ids.shape[0], dtype=jnp.int32)
    earlier = (places[None, :] < places[:, None]).astype(jnp.bfloat16)
    before = jnp.dot(earlier, onehot, preferred_element_type=jnp.float32)
    slot_index = jnp.sum(before * onehot.astype(jnp.float32), axis=1).astype(jnp.int32)
    targets = (expert_ids * capacity + slot_index).reshape(tok_rows, route_count)
    hits = targets[:, :, None] == jnp.arange(experts * capacity, dtype=jnp.int32)[None, None, :]
    spread = jnp.any(hits, axis=1).astype(jnp.bfloat16)
    gains = jnp.sum(jnp.where(hits, route_weight[:, :, None], 0.0), axis=1)
    summed_heads = lax.psum(partial_value, "mp")
    stream = (residual_in.astype(jnp.float32) + summed_heads).astype(jnp.bfloat16)
    own_stream = lax.dynamic_slice_in_dim(stream, col_start, quarter, 1)
    normed_rows = normalize(stream, norm_gain)
    buffer = lax.dot_general(
        spread, normed_rows, (((0,), (0,)), ((), ())), preferred_element_type=jnp.float32
    ).astype(jnp.bfloat16)
    results = run_experts(
        lax.all_to_all(
            buffer.reshape(experts, capacity, model_width),
            "dp",
            split_axis=0,
            concat_axis=0,
            tiled=True,
        ),
        w_gate,
        w_up,
        w_down,
    )
    shared_out = shared_experts(normed_rows, shared_gate, shared_up, shared_down)
    result_rows = results.reshape(experts * capacity, quarter)
    mixture = jnp.dot(gains, result_rows.astype(jnp.float32), precision=lax.Precision.HIGHEST)
    return (own_stream.astype(jnp.float32) + shared_out.astype(jnp.float32) + mixture).astype(
        jnp.bfloat16
    )


def solution(mesh):
    return jax.shard_map(
        on_device,
        mesh=mesh,
        in_specs=(
            P("dp", "mp"),
            P("dp", None, "mp"),
            P("dp", None, None, "mp"),
            P("dp", None),
            P("dp"),
            P("dp", None, None),
            P("mp", None),
            P("dp", None),
            P(),
            P("dp", None),
            P("dp", None),
            P("dp", None, "mp"),
            P("dp", None, "mp"),
            P("dp", None, "mp"),
            P("dp", "mp"),
            P("dp", "mp"),
            P("mp", "dp"),
        ),
        out_specs=P("dp", "mp"),
        check_vma=False,
    )
```

```python
import functools

import jax
import jax.numpy as jnp
from jax import lax
from jax.experimental import pallas as pl
from jax.experimental.pallas import tpu as pltpu
from jax.sharding import PartitionSpec as P

MESH = pl.DeviceIdType.MESH

NEGATIVE_FILL = -1e30
EPSILON = 1e-05
LOG2_E = 1.4426950408889634


def normalize(rows, gain):
    values = rows.astype(jnp.float32)
    mean_square = jnp.mean(values * values, axis=-1, keepdims=True)
    return (values * lax.rsqrt(mean_square + EPSILON) * gain).astype(jnp.bfloat16)


def attend_kernel(
    heads,
    group,
    score_scale,
    table_ref,
    length_ref,
    query_ref,
    fresh_ref,
    mask_ref,
    cache_ref,
    weight_ref,
    out_ref,
    attended,
):
    req_count, tree_len = mask_ref.shape[0], mask_ref.shape[1]
    page, dim = cache_ref.shape[2], cache_ref.shape[3]
    factor = score_scale * LOG2_E
    contract = (((1,), (1,)), ((), ()))
    for r in range(req_count):
        tokens = slice(r * tree_len, (r + 1) * tree_len)
        queries = jnp.concatenate(
            [query_ref[tokens, h * dim : (h + 1) * dim] for h in range(heads)], axis=0
        )
        allow = jnp.concatenate([mask_ref[r]] * heads, axis=0) == 1
        scores = (
            lax.dot_general(
                queries, fresh_ref[tokens, :dim], contract, preferred_element_type=jnp.float32
            )
            * factor
        )
        scores = jnp.where(allow, scores, NEGATIVE_FILL)
        peak = jnp.max(scores, axis=1, keepdims=True)
        probs = jnp.where(allow, jnp.exp2(scores - peak), 0.0)
        denom = jnp.sum(probs, axis=1, keepdims=True)
        weighted = jnp.dot(
            probs.astype(jnp.bfloat16),
            fresh_ref[tokens, dim:],
            preferred_element_type=jnp.float32,
        )
        length = length_ref[r]

        def step(j, carry):
            peak, denom, weighted = carry
            slots = [table_ref[r, j * group + i] for i in range(group)]
            keys = jnp.concatenate([cache_ref[slot, 0] for slot in slots], axis=0)
            values = jnp.concatenate([cache_ref[slot, 1] for slot in slots], axis=0)
            scores = (
                lax.dot_general(queries, keys, contract, preferred_element_type=jnp.float32)
                * factor
            )
            places = lax.broadcasted_iota(jnp.int32, (1, group * page), 1) + j * (group * page)
            scores = jnp.where(places < length, scores, NEGATIVE_FILL)
            new_peak = jnp.maximum(peak, jnp.max(scores, axis=1, keepdims=True))
            probs = jnp.exp2(scores - new_peak)
            shrink = jnp.exp2(peak - new_peak)
            denom = denom * shrink + jnp.sum(probs, axis=1, keepdims=True)
            weighted = weighted * shrink + jnp.dot(
                probs.astype(jnp.bfloat16), values, preferred_element_type=jnp.float32
            )
            return new_peak, denom, weighted

        steps = (length + group * page - 1) // (group * page)
        peak, denom, weighted = lax.fori_loop(0, steps, step, (peak, denom, weighted))
        result = (weighted / denom).astype(jnp.bfloat16)
        for h in range(heads):
            attended[tokens, h * dim : (h + 1) * dim] = result[h * tree_len : (h + 1) * tree_len]
    out_ref[...] = jnp.dot(
        attended[...], weight_ref[...], preferred_element_type=jnp.float32
    ).astype(out_ref.dtype)


def attend(
    tree_query, new_kv, kv_cache, page_table, cache_len, tree_mask, out_weight, out_dtype
):
    tok_rows, dim = tree_query.shape[0], new_kv.shape[2]
    heads = tree_query.shape[1] // dim
    group = 4 if page_table.shape[1] % 4 == 0 else 1
    vmem, smem = pl.BlockSpec(memory_space=pltpu.VMEM), pl.BlockSpec(memory_space=pltpu.SMEM)
    return pl.pallas_call(
        functools.partial(attend_kernel, heads, group, dim ** (-0.5)),
        out_shape=jax.ShapeDtypeStruct((tok_rows, out_weight.shape[1]), out_dtype),
        in_specs=[smem, smem, vmem, vmem, vmem, vmem, vmem],
        out_specs=vmem,
        scratch_shapes=[pltpu.VMEM(tree_query.shape, jnp.bfloat16)],
        compiler_params=pltpu.CompilerParams(vmem_limit_bytes=24 * 1024 * 1024),
        cost_estimate=pl.CostEstimate(
            flops=1_000_000_000, bytes_accessed=6_000_000, transcendentals=1_200_000
        ),
        name="attend",
    )(
        page_table,
        cache_len,
        tree_query,
        new_kv.reshape(tok_rows, 2 * dim),
        tree_mask,
        kv_cache,
        out_weight,
    )


def run_experts(rows, w_gate, w_up, w_down):
    source_count, slot_count, model_width = rows.shape
    flat_rows = rows.reshape(source_count * slot_count, model_width)
    gate_proj = jnp.dot(flat_rows, w_gate[0], preferred_element_type=jnp.float32)
    up_proj = jnp.dot(flat_rows, w_up[0], preferred_element_type=jnp.float32)
    hidden_act = (jax.nn.silu(gate_proj) * up_proj).astype(jnp.bfloat16)
    down_rows = w_down[0]
    summed = jnp.dot(
        lax.all_gather(hidden_act, "mp", axis=1, tiled=True),
        down_rows,
        preferred_element_type=jnp.float32,
    )
    outputs = summed.astype(jnp.bfloat16).reshape(source_count, slot_count, w_down.shape[2])
    return lax.all_to_all(outputs, "dp", split_axis=0, concat_axis=0, tiled=True)


def shared_experts(normed_rows, shared_gate, shared_up, shared_down):
    gate_total = jnp.dot(
        normed_rows,
        lax.all_gather(shared_gate, "dp", axis=0, tiled=True),
        preferred_element_type=jnp.float32,
    )
    up_total = jnp.dot(
        normed_rows,
        lax.all_gather(shared_up, "dp", axis=0, tiled=True),
        preferred_element_type=jnp.float32,
    )
    shared_hidden = (jax.nn.silu(gate_total) * up_total).astype(jnp.bfloat16)
    terms = jnp.dot(
        shared_hidden,
        lax.all_gather(shared_down, "dp", axis=1, tiled=True),
        preferred_element_type=jnp.float32,
    )
    return lax.psum_scatter(terms.astype(jnp.bfloat16), "mp", scatter_dimension=1, tiled=True)


def mp_relations(m):
    x, c = m // 2, m % 2
    return (x * 2 + (1 - c), (1 - x) * 2 + c, (1 - x) * 2 + (1 - c))


def remote(src, dst, send, recv, device):
    return pltpu.make_async_remote_copy(
        src_ref=src, dst_ref=dst, send_sem=send, recv_sem=recv, device_id=device, device_id_type=MESH
    )


def greet(devices):
    barrier = pltpu.get_barrier_semaphore()
    for device in devices:
        pl.semaphore_signal(barrier, inc=1, device_id=device, device_id_type=MESH)
    pl.semaphore_wait(barrier, len(devices))


def norm_gather_kernel(
    n_dp,
    partial_ref,
    residual_ref,
    gain_ref,
    rows_ref,
    stream_ref,
    terms,
    stream_own,
    normed_own,
    rs_send,
    rs_recv,
    st_send,
    st_recv,
    dp_send,
    dp_recv,
    x_send,
    x_recv,
    c_send,
    c_recv,
    r_send,
    r_recv,
    local_sem,
):
    d, m = lax.axis_index("dp"), lax.axis_index("mp")
    mates = mp_relations(m)
    core_mate, x_mate = mates[0], mates[1]
    peers = [lax.rem(d + k, n_dp) for k in range(1, n_dp)]
    greet([(d, mate) for mate in mates] + [(peer, m) for peer in peers])
    quarter = stream_own.shape[2]
    rs_copies = [
        remote(partial_ref.at[mate], terms.at[i], rs_send.at[i], rs_recv.at[i], (d, mate))
        for i, mate in enumerate(mates)
    ]
    for copy in (rs_copies[1], rs_copies[2], rs_copies[0]):
        copy.start()
    total = residual_ref[...].astype(jnp.float32) + partial_ref[m].astype(jnp.float32)
    for i, copy in enumerate(rs_copies):
        copy.wait_recv()
        total = total + terms[i].astype(jnp.float32)
    stream = total.astype(jnp.bfloat16)
    values = stream.astype(jnp.float32)
    mean_square = jnp.mean(values * values, axis=-1, keepdims=True)
    normed_own[...] = (values * lax.rsqrt(mean_square + EPSILON) * gain_ref[...]).astype(
        jnp.bfloat16
    )
    for i in range(4):
        stream_own[i] = stream[:, i * quarter : (i + 1) * quarter]
    dp_copies = [
        remote(normed_own, rows_ref.at[d, m], dp_send.at[k], dp_recv.at[k], (peers[k], m))
        for k in range(n_dp - 1)
    ]
    for copy in dp_copies:
        copy.start()
    x_copies, c_copies, r_copies = [], [], []

    def forward(k, source):
        owner = lax.rem(d + n_dp - k, n_dp)
        x_copy = remote(source, rows_ref.at[owner, m], x_send.at[k], x_recv.at[k], (d, x_mate))
        c_copy = remote(source, rows_ref.at[owner, m], c_send.at[k], c_recv.at[k], (d, core_mate))
        x_copy.start()
        c_copy.start()
        x_copies.append(x_copy)
        c_copies.append(c_copy)

    def relay(k):
        owner = lax.rem(d + n_dp - k, n_dp)
        x_copies[k].wait_recv()
        block = rows_ref.at[owner, x_mate]
        copy = remote(block, block, r_send.at[k], r_recv.at[k], (d, core_mate))
        copy.start()
        r_copies.append(copy)

    forward(0, normed_own)
    own_rows = pltpu.make_async_copy(normed_own, rows_ref.at[d, m], local_sem.at[0])
    own_rows.start()
    own_stream = pltpu.make_async_copy(stream_own.at[m], stream_ref.at[m], local_sem.at[1])
    own_stream.start()
    st_copies = [
        remote(stream_own.at[mate], stream_ref.at[m], st_send.at[i], st_recv.at[i], (d, mate))
        for i, mate in enumerate(mates)
    ]
    for copy in st_copies:
        copy.start()
    for k in range(1, n_dp):
        dp_copies[k - 1].wait_recv()
        forward(k, rows_ref.at[lax.rem(d + n_dp - k, n_dp), m])
        relay(k - 1)
    relay(n_dp - 1)
    own_rows.wait()
    own_stream.wait()
    for copy in rs_copies + dp_copies + x_copies:
        copy.wait_send()
    for copy in st_copies + c_copies + r_copies:
        copy.wait()


def norm_gather(n_dp, partial, residual, gain):
    rows, width = residual.shape
    dma = pltpu.SemaphoreType.DMA
    return pl.pallas_call(
        functools.partial(norm_gather_kernel, n_dp),
        out_shape=(
            jax.ShapeDtypeStruct((n_dp, 4, rows, width), jnp.bfloat16),
            jax.ShapeDtypeStruct((4, rows, width // 4), jnp.bfloat16),
        ),
        in_specs=[pl.BlockSpec(memory_space=pltpu.VMEM)] * 3,
        out_specs=(pl.BlockSpec(memory_space=pl.ANY),) * 2,
        scratch_shapes=[
            pltpu.VMEM((3, rows, width), jnp.bfloat16),
            pltpu.VMEM((4, rows, width // 4), jnp.bfloat16),
            pltpu.VMEM((rows, width), jnp.bfloat16),
            dma((3,)),
            dma((3,)),
            dma((3,)),
            dma((3,)),
            dma((n_dp - 1,)),
            dma((n_dp - 1,)),
            dma((n_dp,)),
            dma((n_dp,)),
            dma((n_dp,)),
            dma((n_dp,)),
            dma((n_dp,)),
            dma((n_dp,)),
            dma((2,)),
        ],
        compiler_params=pltpu.CompilerParams(
            collective_id=0, has_side_effects=True, vmem_limit_bytes=16 * 1024 * 1024
        ),
        name="norm_gather",
    )(partial, residual, gain)


def expert_kernel(
    n_dp,
    units,
    rows_ref,
    scale_ref,
    gate_ref,
    up_ref,
    down_ref,
    terms_ref,
    hidden,
    outputs,
    x_send,
    x_recv,
    c_send,
    c_recv,
    r_send,
    r_recv,
    dp_send,
    dp_recv,
):
    d, m = lax.axis_index("dp"), lax.axis_index("mp")
    core_mate, x_mate, _ = mp_relations(m)
    greet(
        [(d, core_mate), (d, x_mate)] + [(lax.rem(d + k, n_dp), m) for k in range(1, n_dp)]
    )
    relay_lag, finish_lag = 2, 4
    width = gate_ref.shape[1]

    def block_of(k):
        return lax.rem(d + k + 1, n_dp)

    def x_copy(k):
        block = hidden.at[m, block_of(k)]
        return remote(block, block, x_send.at[k], x_recv.at[k], (d, x_mate))

    def c_copy(k):
        block = hidden.at[m, block_of(k)]
        return remote(block, block, c_send.at[k], c_recv.at[k], (d, core_mate))

    def r_copy(k):
        block = hidden.at[x_mate, block_of(k)]
        return remote(block, block, r_send.at[k], r_recv.at[k], (d, core_mate))

    def dp_copy(k):
        t = block_of(k)
        return remote(outputs.at[t], terms_ref.at[d], dp_send.at[k], dp_recv.at[k], (t, m))

    def step(s, carry):
        @pl.when(s < n_dp)
        def _():
            t = block_of(s)
            rows = rows_ref[t]
            gate = jnp.dot(rows, gate_ref[...], preferred_element_type=jnp.float32)
            up = jnp.dot(rows, up_ref[...], preferred_element_type=jnp.float32)
            routed = lax.broadcasted_iota(jnp.int32, (1, width), 1) < units
            scale = jnp.where(routed, scale_ref[t], 1.0)
            hidden[m, t] = (jax.nn.silu(gate) * up * scale).astype(jnp.bfloat16)
            x_copy(s).start()
            c_copy(s).start()

        @pl.when((s >= relay_lag) & (s < n_dp + relay_lag))
        def _():
            x_copy(s - relay_lag).wait_recv()
            r_copy(s - relay_lag).start()

        @pl.when(s >= finish_lag)
        def _():
            k = s - finish_lag
            t = block_of(k)
            c_copy(k).wait_recv()
            r_copy(k).wait_recv()
            total = jnp.dot(hidden[0, t], down_ref[0], preferred_element_type=jnp.float32)
            for i in range(1, 4):
                total += jnp.dot(hidden[i, t], down_ref[i], preferred_element_type=jnp.float32)
            result = total.astype(jnp.bfloat16)

            @pl.when(k < n_dp - 1)
            def _():
                outputs[t] = result
                dp_copy(k).start()

            @pl.when(k == n_dp - 1)
            def _():
                terms_ref[d] = result

        return carry

    lax.fori_loop(0, n_dp + finish_lag, step, 0)

    def finish(k, carry):
        x_copy(k).wait_send()
        c_copy(k).wait_send()
        r_copy(k).wait_send()

        @pl.when(k < n_dp - 1)
        def _():
            dp_copy(k).wait()

        return carry

    lax.fori_loop(0, n_dp, finish, 0)


def run_blocks(units, rows, scale, gate, up, down):
    n_dp, tok_rows, _ = rows.shape
    width, columns = gate.shape[1], down.shape[2]
    vmem, dma = pl.BlockSpec(memory_space=pltpu.VMEM), pltpu.SemaphoreType.DMA
    return pl.pallas_call(
        functools.partial(expert_kernel, n_dp, units),
        out_shape=jax.ShapeDtypeStruct((n_dp, tok_rows, columns), jnp.bfloat16),
        in_specs=[vmem] * 5,
        out_specs=vmem,
        scratch_shapes=[
            pltpu.VMEM((4, n_dp, tok_rows, width), jnp.bfloat16),
            pltpu.VMEM((n_dp, tok_rows, columns), jnp.bfloat16),
        ]
        + [dma((n_dp,))] * 6
        + [dma((n_dp - 1,))] * 2,
        compiler_params=pltpu.CompilerParams(
            collective_id=1, has_side_effects=True, vmem_limit_bytes=40 * 1024 * 1024
        ),
        name="run_blocks",
    )(rows, scale, gate, up, down)


def split_three(values):
    pieces = []
    for _ in range(3):
        piece = lax.reduce_precision(values, 8, 7)
        pieces.append(piece.astype(jnp.bfloat16))
        values = values - piece
    return pieces


def shared_slices(shared_gate, shared_up, shared_down, by_expert):
    n_dp = lax.axis_size("dp")
    depth, units = shared_gate.shape
    share = units // n_dp
    pieces = jnp.stack(split_three(by_expert), axis=1)
    pieces = jnp.pad(pieces, ((0, 0), (0, 5), (0, depth - pieces.shape[2])))
    parts = jnp.concatenate(
        [
            shared_gate.T.reshape(n_dp, share, depth),
            shared_up.T.reshape(n_dp, share, depth),
            shared_down.reshape(n_dp, share, depth),
            pieces,
        ],
        axis=1,
    )
    parts = lax.all_to_all(parts, "dp", split_axis=0, concat_axis=0, tiled=True)
    row_scale = jnp.sum(
        parts[:, 3 * share : 3 * share + 3, : by_expert.shape[1]].astype(jnp.float32), axis=1
    )
    parts = parts[:, : 3 * share].transpose(1, 0, 2).reshape(3, share, n_dp * depth)
    down = parts[2].reshape(share, 4, -1).transpose(1, 0, 2)
    down = lax.all_to_all(down, "mp", split_axis=0, concat_axis=0, tiled=True)
    return parts[0].T, parts[1].T, down, row_scale


def dense_tail(
    partial_value,
    residual_in,
    norm_gain,
    route_ids,
    route_weight,
    w_gate,
    w_up,
    w_down,
    shared_gate,
    shared_up,
    shared_down,
):
    n_dp = lax.axis_size("dp")
    tok_rows, model_width = residual_in.shape
    units = w_gate.shape[2]
    chosen = route_ids[None, :, :] == jnp.arange(n_dp, dtype=jnp.int32)[:, None, None]
    by_expert = jnp.sum(jnp.where(chosen, route_weight[None], 0.0), axis=2)
    own_gate, own_up, own_down, row_scale = shared_slices(
        shared_gate, shared_up, shared_down, by_expert
    )
    share = own_gate.shape[1]
    width = -(-(units + share) // 128) * 128
    spare = width - units - share
    columns_pad = jnp.zeros((model_width, spare), jnp.bfloat16)
    gate_all = jnp.concatenate([w_gate[0], own_gate, columns_pad], axis=1)
    up_all = jnp.concatenate([w_up[0], own_up, columns_pad], axis=1)
    down_width = w_down.shape[2]
    down_all = jnp.concatenate(
        [
            w_down[0].reshape(4, units, down_width),
            own_down,
            jnp.zeros((4, spare, down_width), jnp.bfloat16),
        ],
        axis=1,
    )
    row_scale = row_scale.reshape(n_dp, tok_rows, 1)
    slice_rows = tok_rows // 4
    own_start = lax.axis_index("mp") * slice_rows
    rows, stream = norm_gather(
        n_dp,
        partial_value.reshape(4, slice_rows, model_width),
        lax.dynamic_slice_in_dim(residual_in, own_start, slice_rows, 0),
        norm_gain.reshape(1, model_width),
    )
    rows = rows.reshape(n_dp, tok_rows, model_width)
    terms = run_blocks(units, rows, row_scale, gate_all, up_all, down_all)
    total = stream.reshape(tok_rows, down_width).astype(jnp.float32)
    return (total + jnp.sum(terms.astype(jnp.float32), axis=0)).astype(jnp.bfloat16)


def on_device(
    tree_query,
    new_kv,
    kv_cache,
    page_table,
    cache_len,
    tree_mask,
    out_weight,
    residual_in,
    norm_gain,
    route_ids,
    route_weight,
    w_gate,
    w_up,
    w_down,
    shared_gate,
    shared_up,
    shared_down,
):
    tok_rows = tree_query.shape[0]
    experts = lax.axis_size("dp") * w_gate.shape[0]
    route_count = route_ids.shape[1]
    capacity = min(tok_rows, 4 * tok_rows * route_count // (3 * experts))
    every_row = capacity == tok_rows and w_gate.shape[0] == 1 and lax.axis_size("mp") == 4
    partial_value = attend(
        tree_query,
        new_kv,
        kv_cache,
        page_table,
        cache_len,
        tree_mask,
        out_weight,
        jnp.bfloat16 if every_row else jnp.float32,
    )
    model_width = residual_in.shape[1]
    quarter = model_width // lax.axis_size("mp")
    col_start = lax.axis_index("mp") * quarter
    if every_row:
        return dense_tail(
            partial_value,
            residual_in,
            norm_gain,
            route_ids,
            route_weight,
            w_gate,
            w_up,
            w_down,
            shared_gate,
            shared_up,
            shared_down,
        )
    expert_ids = route_ids.reshape(-1)
    onehot = expert_ids[:, None] == jnp.arange(experts, dtype=jnp.int32)[None, :]
    onehot = onehot.astype(jnp.bfloat16)
    places = jnp.arange(expert_ids.shape[0], dtype=jnp.int32)
    earlier = (places[None, :] < places[:, None]).astype(jnp.bfloat16)
    before = jnp.dot(earlier, onehot, preferred_element_type=jnp.float32)
    slot_index = jnp.sum(before * onehot.astype(jnp.float32), axis=1).astype(jnp.int32)
    targets = (expert_ids * capacity + slot_index).reshape(tok_rows, route_count)
    hits = targets[:, :, None] == jnp.arange(experts * capacity, dtype=jnp.int32)[None, None, :]
    spread = jnp.any(hits, axis=1).astype(jnp.bfloat16)
    gains = jnp.sum(jnp.where(hits, route_weight[:, :, None], 0.0), axis=1)
    summed_heads = lax.psum(partial_value, "mp")
    stream = (residual_in.astype(jnp.float32) + summed_heads).astype(jnp.bfloat16)
    own_stream = lax.dynamic_slice_in_dim(stream, col_start, quarter, 1)
    normed_rows = normalize(stream, norm_gain)
    buffer = lax.dot_general(
        spread, normed_rows, (((0,), (0,)), ((), ())), preferred_element_type=jnp.float32
    ).astype(jnp.bfloat16)
    results = run_experts(
        lax.all_to_all(
            buffer.reshape(experts, capacity, model_width),
            "dp",
            split_axis=0,
            concat_axis=0,
            tiled=True,
        ),
        w_gate,
        w_up,
        w_down,
    )
    shared_out = shared_experts(normed_rows, shared_gate, shared_up, shared_down)
    result_rows = results.reshape(experts * capacity, quarter)
    mixture = jnp.dot(gains, result_rows.astype(jnp.float32), precision=lax.Precision.HIGHEST)
    return (own_stream.astype(jnp.float32) + shared_out.astype(jnp.float32) + mixture).astype(
        jnp.bfloat16
    )


def solution(mesh):
    return jax.shard_map(
        on_device,
        mesh=mesh,
        in_specs=(
            P("dp", "mp"),
            P("dp", None, "mp"),
            P("dp", None, None, "mp"),
            P("dp", None),
            P("dp"),
            P("dp", None, None),
            P("mp", None),
            P("dp", None),
            P(),
            P("dp", None),
            P("dp", None),
            P("dp", None, "mp"),
            P("dp", None, "mp"),
            P("dp", None, "mp"),
            P("dp", "mp"),
            P("dp", "mp"),
            P("mp", "dp"),
        ),
        out_specs=P("dp", "mp"),
        check_vma=False,
    )
```
